32 devices in a mesh: section: 2 (over y), hid: 4 (over x, core), dp: 4 (over z).
Axes of the slice: x: 2, y: 2, z: 4, core: 2. Of those that a mesh axis runs over, the one named last changes fastest.
Arguments:
- acts_in: bfloat16 [2, 2, 512, 8192], P('section', None, 'dp', 'hid'), may hold values from -6 to 6
- pre_act: bfloat16 [2, 2, 512, 16384], P('section', None, 'dp', 'hid'), may hold values from -6 to 6
- out_grad: bfloat16 [2, 512, 8192], P(None, 'dp', 'hid'), may hold values from -6 to 6
- up_weight: bfloat16 [2, 3, 64, 256, 256], P('section', None, 'hid'), may hold values from -0.21875 to 0.21875
- down_weight: bfloat16 [2, 3, 64, 256, 256], P('section', None, 'hid'), may hold values from -0.21875 to 0.21875
- up_pick: int32 [2, 3, 64], P('section', None, 'hid'), may hold values from 0 to 7
- down_pick: int32 [2, 3, 64], P('section', None, 'hid'), may hold values from 0 to 7
- factor_order: int32 [2, 3], P('section'), may hold values from 0 to 2, each once within a row
Outputs:
- grad_in: bfloat16 [2, 2, 512, 8192], P('section', None, 'dp', 'hid')
- up_grad: float32 [2, 3, 64, 256, 256], P('section', None, 'hid', 'dp')
- down_grad: float32 [2, 3, 64, 256, 256], P('section', None, 'hid', None, 'dp')
The draws below stay inside these ranges and needn't reach their ends.
Inputs may be any that keep to these rules, and one draw needn't show every extreme that they name: Each row of factor_order names each of the 3 weight slots once.
All inputs are finite; a program needn't handle non-finite values.
Results may differ from the reference program's by a relative error of at most 0.019.
Values may be sent and summed in bfloat16 or wider, within the bound.
No kernel may reach another device: no remote copies, remote signals or barrier semaphores. Data moves between devices by JAX's collectives and lax.ppermute only.
A program may use at most 128 MiB of HBM per device.

```python
import jax
import jax.numpy as jnp
import numpy as np
from jax import lax

D = 8192
H = 16384
BLK = 256
MICRO = 2
BITS = 2
F = 3
FB_DEV = 8
HB = 64
TOKENS = 512
N_SECTION = 2
N_HID = 4


def place_ends(drawn, key, low, top_value):
    shape = drawn.shape
    index_at = [jax.random.randint(jax.random.fold_in(key, axis), (), 0, shape[axis]) for axis in range(len(shape))]
    drawn = drawn.at[tuple(index_at)].set(low)
    longest = shape.index(max(shape))
    index_at[longest] = (index_at[longest] + 1) % shape[longest]
    return drawn.at[tuple(index_at)].set(top_value)


def level_of(rng, dims, pieces, least, high):
    def one(axis_at, shards_of):
        draws = jax.random.uniform(jax.random.fold_in(jax.random.fold_in(rng, 6), axis_at), (shards_of,), jnp.float32, least / len(pieces), high / len(pieces))
        return jnp.repeat(jnp.exp(draws), dims[axis_at] // shards_of).reshape((-1,) + (1,) * (len(dims) - axis_at - 1))

    loudness = one(*pieces[0])
    for cut in pieces[1:]:
        loudness = loudness * one(*cut)
    return loudness


def gaussian(stream_key, shape, width, limit, split=(), held_as=jnp.bfloat16):
    array = jax.random.normal(stream_key, shape, jnp.float32) * width
    if len(split) > 0:
        array = level_of(stream_key, shape, split, -0.22, 0.18) * array
    return jnp.clip(array, min=-limit, max=limit).astype(held_as)


def setup_inputs(seed: int = 0) -> dict:
    key_list = jax.random.split(jax.random.key(seed), 9)
    acts_in = gaussian(key_list[0], (N_SECTION, MICRO, TOKENS, D), 1.0, 6.0, ((0, 2), (2, 4), (3, 4)))
    pre_act = gaussian(key_list[1], (N_SECTION, MICRO, TOKENS, H), 1.0, 6.0, ((0, 2), (2, 4), (3, 4)))
    out_grad = gaussian(key_list[2], (MICRO, TOKENS, D), 1.0, 6.0, ((1, 4), (2, 4)))
    up_weight = gaussian(key_list[3], (N_SECTION, F, HB, BLK, BLK), (F * BLK) ** -0.5, 0.21875, ((0, 2), (2, 4)))
    down_weight = gaussian(key_list[4], (N_SECTION, F, HB, BLK, BLK), (F * BLK) ** -0.5, 0.21875, ((0, 2), (2, 4)))
    up_pick = place_ends(jax.random.randint(key_list[5], (N_SECTION, F, HB), 0, FB_DEV), jax.random.fold_in(key_list[5], 1), 0, FB_DEV - 1).astype(jnp.int32)
    down_pick = place_ends(jax.random.randint(key_list[6], (N_SECTION, F, HB), 0, FB_DEV), jax.random.fold_in(key_list[6], 1), 0, FB_DEV - 1).astype(jnp.int32)
    factor_order = jax.vmap(lambda own: jax.random.permutation(own, F))(jax.random.split(key_list[7], N_SECTION)).reshape((N_SECTION, F)).astype(jnp.int32)
    return {"acts_in": acts_in, "pre_act": pre_act, "out_grad": out_grad, "up_weight": up_weight, "down_weight": down_weight, "up_pick": up_pick, "down_pick": down_pick, "factor_order": factor_order}


def gelu_tanh(values):
    return jax.nn.gelu(values, approximate=True)

def gelu_slope(values, pull_in):
    _, pull_back = jax.vjp(gelu_tanh, values)
    return pull_back(pull_in)[0]

def reference(acts_in, pre_act, out_grad, up_weight, down_weight, up_pick, down_pick, factor_order):
    highest = lax.Precision.HIGHEST
    groups = N_HID
    fgroup = D // (BLK * groups)
    hgroup = H // (BLK * groups)
    factor_count = BITS + 1
    partner = [np.arange(groups)] + [np.arange(groups) ^ 1 << bit_number for bit_number in range(BITS)]
    grad_now = out_grad
    grad_list = [None] * N_SECTION
    up_list = [None] * N_SECTION
    down_list = [None] * N_SECTION
    for layer_index in range(N_SECTION - 1, -1, -1):
        order_index = factor_order[layer_index].astype(jnp.int32)
        w_up = up_weight[layer_index][order_index].reshape(factor_count, groups, hgroup, BLK, BLK)
        w_down = down_weight[layer_index][order_index].reshape(factor_count, groups, hgroup, BLK, BLK)
        pick_up = up_pick[layer_index][order_index].reshape(factor_count, groups, hgroup)
        pick_down = down_pick[layer_index][order_index].reshape(factor_count, groups, hgroup)
        up_acc = jnp.zeros((factor_count, groups, hgroup, BLK, BLK), jnp.float32)
        down_acc = jnp.zeros((factor_count, groups, hgroup, BLK, BLK), jnp.float32)
        new_grad = []
        for micro_index in range(MICRO):
            g_blocks = grad_now[micro_index].reshape(TOKENS, groups, fgroup, BLK)
            input_now = acts_in[layer_index, micro_index].reshape(TOKENS, groups, fgroup, BLK)
            pre_now = pre_act[layer_index, micro_index].astype(jnp.float32).reshape(TOKENS, groups, hgroup, BLK)
            slope_in = jnp.zeros(pre_now.shape, jnp.float32)
            picked = []
            for factor in range(factor_count):
                source = g_blocks[:, partner[factor]]
                chosen = jnp.take_along_axis(source, pick_down[factor][None, :, :, None], axis=2)
                picked.append(chosen)
                slope_in = slope_in + jnp.einsum('tijc,ijdc->tijd', chosen.astype(jnp.float32), w_down[factor].astype(jnp.float32), precision=highest)
            hidden_grad = gelu_slope(pre_now, slope_in).astype(jnp.bfloat16)
            active = gelu_tanh(pre_now).astype(jnp.bfloat16)
            summed = g_blocks.astype(jnp.float32)
            for factor in range(factor_count):
                down_acc = down_acc.at[factor].add(jnp.einsum('tijd,tijc->ijdc', active.astype(jnp.float32), picked[factor].astype(jnp.float32), precision=highest))
                chosen_x = jnp.take_along_axis(input_now[:, partner[factor]], pick_up[factor][None, :, :, None], axis=2)
                up_acc = up_acc.at[factor].add(jnp.einsum('tijc,tijd->ijcd', chosen_x.astype(jnp.float32), hidden_grad.astype(jnp.float32), precision=highest))
                product = jnp.einsum('tijd,ijcd->tijc', hidden_grad.astype(jnp.float32), w_up[factor].astype(jnp.float32), precision=highest)
                onehot = (pick_up[factor][:, :, None] == jnp.arange(fgroup, dtype=jnp.int32)[None, None, :]).astype(jnp.float32)
                returned = jnp.einsum('tijc,ije->tiec', product, onehot, precision=highest)
                if factor == 0:
                    summed = summed + returned
                else:
                    rounded = lax.optimization_barrier(returned.astype(jnp.bfloat16)).astype(jnp.float32)
                    summed = summed + rounded[:, partner[factor]]
            new_grad.append(summed.astype(jnp.bfloat16).reshape(TOKENS, D))
        grad_now = jnp.stack(new_grad)
        grad_list[layer_index] = grad_now
        up_list[layer_index] = jnp.zeros_like(up_acc).at[order_index].set(up_acc).reshape(factor_count, H // BLK, BLK, BLK)
        down_list[layer_index] = jnp.zeros_like(down_acc).at[order_index].set(down_acc).reshape(factor_count, H // BLK, BLK, BLK)
    return (jnp.stack(grad_list), jnp.stack(up_list), jnp.stack(down_list))
```

```python
import functools
import itertools

import jax
import jax.numpy as jnp
from jax import lax
from jax.experimental import pallas as pl
from jax.experimental.pallas import tpu as pltpu
from jax.sharding import PartitionSpec as P

AXES = ("section", "hid", "dp")
VMEM_LIMIT = 52 * 1024 * 1024
ROOT = 0.7978845608028654
CUBE = 0.044715
F32 = jnp.float32
BF16 = jnp.bfloat16


def send(value, target):
    sizes = [lax.axis_size(axis) for axis in AXES]

    def flat(at):
        return (at[0] * sizes[1] + at[1]) * sizes[2] + at[2]

    route = []
    for at in itertools.product(*(range(size) for size in sizes)):
        to = target(*at)
        if to is not None:
            route.append((flat(at), flat(to)))
    return lax.ppermute(value, AXES, route)


def end_to_near(value):
    return send(value, lambda s, h, z: {0: (s, h, 1), 3: (s, h, 2)}.get(z))


def end_to_far(value):
    return send(value, lambda s, h, z: {0: (s, h, 2), 3: (s, h, 1)}.get(z))


def near_to_end(value):
    return send(value, lambda s, h, z: {1: (s, h, 0), 2: (s, h, 3)}.get(z))


def mid_to_far(value):
    return send(value, lambda s, h, z: {1: (s, h, 3), 2: (s, h, 0)}.get(z))


def mid_swap(value):
    return send(value, lambda s, h, z: {1: (s, h, 2), 2: (s, h, 1)}.get(z))


def mid_partner(value, bit):
    return send(value, lambda s, h, z: (s, h ^ 1 << bit, z) if z in (1, 2) else None)


def section_partner(value, bit, active):
    return send(value, lambda s, h, z: (s, h ^ 1 << bit, z) if s == active else None)


def section_down(value, active):
    return send(value, lambda s, h, z: (s - 1, h, z) if s == active else None)


def chain_body(factors, steps, per_step, blk, fgroup, info, pick_up, pick_down, *refs):
    g_refs, refs = refs[:factors], refs[factors:]
    pre_ref, refs = refs[0], refs[1:]
    down_refs, refs = refs[:factors], refs[factors:]
    up_refs, refs = refs[:factors], refs[factors:]
    du_old, gm_old, go_old = refs[:3]
    du_ref, gm_ref, go_ref, own_ref = refs[3:7]
    cross_refs, total = refs[7:-1], refs[-1]
    hgroup = steps * per_step
    half_width = blk // 2
    step = pl.program_id(0)
    active = info[0] == 1

    @pl.when(jnp.logical_not(active))
    def _():
        du_ref[...] = du_old[...]

        @pl.when(step == 0)
        def _():
            gm_ref[...] = gm_old[...]
            go_ref[...] = go_old[...]

    @pl.when(active)
    def _():
        @pl.when(step == 0)
        def _():
            total[...] = jnp.zeros_like(total)
            half = info[1]
            for b in range(fgroup):
                mine = pl.ds(pl.multiple_of(b * blk + half * half_width, half_width), half_width)
                other = pl.ds(
                    pl.multiple_of(b * blk + (1 - half) * half_width, half_width), half_width
                )
                place = slice(b * half_width, (b + 1) * half_width)
                for f in range(factors):
                    gm_ref[f, :, place] = g_refs[f][:, mine]
                go_ref[:, place] = g_refs[0][:, other]

        for k in range(per_step):
            j = step * per_step + k
            columns = slice(k * blk, (k + 1) * blk)
            da = None
            for f in range(factors):
                pick = pick_down[info[2 + f] * hgroup + j]
                chosen = g_refs[f][:, pl.ds(pl.multiple_of(pick * blk, blk), blk)]
                part = lax.dot_general(
                    chosen, down_refs[f][0, 0, k], (((1,), (1,)), ((), ())), preferred_element_type=F32
                )
                da = part if da is None else da + part
            v = pre_ref[0, 0, :, columns].astype(F32)
            square = v * v
            t = jnp.tanh(ROOT * v * (1.0 + CUBE * square))
            slope = 0.5 * (1.0 + t) + 0.5 * ROOT * v * (1.0 - t * t) * (1.0 + 3.0 * CUBE * square)
            du = (slope * da).astype(BF16)
            du_ref[0, :, columns] = du
            for f in range(factors):
                pick = pick_up[info[2 + f] * hgroup + j]
                place = pl.ds(pl.multiple_of(pick * blk, blk), blk)
                total[f, :, place] += lax.dot_general(
                    du, up_refs[f][0, 0, k], (((1,), (1,)), ((), ())), preferred_element_type=F32
                )

        @pl.when(step == steps - 1)
        def _():
            own_ref[...] = g_refs[0][...].astype(F32) + total[0]
            for f in range(1, factors):
                cross_refs[f - 1][...] = total[f].astype(BF16)


def chain(info, pick_up, pick_down, g_list, pre_act, down_weight, up_weight, du, gm, go, micro, chunks):
    factors = len(g_list)
    tokens, width = g_list[0].shape
    hgroup, blk = up_weight.shape[2], up_weight.shape[-1]
    fgroup = width // blk
    per_step = hgroup // chunks
    wide = per_step * blk
    whole = pl.BlockSpec((tokens, width), lambda j, *s: (0, 0))

    def weight_spec(f):
        return pl.BlockSpec(
            (1, 1, per_step, blk, blk), lambda j, info, *s: (0, info[2 + f], j * info[0], 0, 0)
        )

    du_spec = pl.BlockSpec((1, tokens, wide), lambda j, *s: (j, micro, 0))
    gm_spec = pl.BlockSpec((factors, tokens, width // 2), lambda j, *s: (0, micro, 0))
    go_spec = pl.BlockSpec((tokens, width // 2), lambda j, *s: (micro, 0))
    pre_spec = pl.BlockSpec((1, 1, tokens, wide), lambda j, info, *s: (0, micro, 0, j * info[0]))
    first_alias = 3 + factors + 1 + 2 * factors
    flat = jax.ShapeDtypeStruct((tokens, width), BF16)
    macs = tokens * hgroup * blk * blk * factors * 2
    return pl.pallas_call(
        functools.partial(chain_body, factors, chunks, per_step, blk, fgroup),
        grid_spec=pltpu.PrefetchScalarGridSpec(
            num_scalar_prefetch=3,
            grid=(chunks,),
            in_specs=[whole] * factors
            + [pre_spec]
            + [weight_spec(f) for f in range(factors)] * 2
            + [du_spec, gm_spec, go_spec],
            out_specs=[du_spec, gm_spec, go_spec, whole] + [whole] * (factors - 1),
            scratch_shapes=[pltpu.VMEM((factors, tokens, width), F32)],
        ),
        out_shape=[
            jax.ShapeDtypeStruct(du.shape, BF16),
            jax.ShapeDtypeStruct(gm.shape, BF16),
            jax.ShapeDtypeStruct(go.shape, BF16),
            jax.ShapeDtypeStruct((tokens, width), F32),
        ]
        + [flat] * (factors - 1),
        input_output_aliases={first_alias: 0, first_alias + 1: 1, first_alias + 2: 2},
        compiler_params=pltpu.CompilerParams(vmem_limit_bytes=VMEM_LIMIT),
        cost_estimate=pl.CostEstimate(
            flops=2 * macs, bytes_accessed=4 * factors * hgroup * blk * blk, transcendentals=0
        ),
        name="chain",
    )(
        info,
        pick_up,
        pick_down,
        *g_list,
        pre_act,
        *[down_weight] * factors,
        *[up_weight] * factors,
        du,
        gm,
        go,
    )


def up_body(factors, count, hgroup, blk, first, info, pick_up, *refs):
    own_x, near_x = refs[:factors], refs[factors : 2 * factors]
    du_own, du_near, mine_ref, near_ref, mid_ref, far_ref, held = refs[2 * factors :]
    quarter = blk // 4
    z = info[0]

    def rows(at):
        return pl.ds(pl.multiple_of(at * quarter, quarter), quarter)

    for k in range(count):
        columns = slice(k * blk, (k + 1) * blk)
        for f in range(factors):
            slot = info[1 + f]
            place = pl.ds(pl.multiple_of(pick_up[slot * hgroup + first + k] * blk, blk), blk)
            held[...] = jnp.dot(
                own_x[f][place, :], du_own[0, :, columns], preferred_element_type=F32
            ) + jnp.dot(near_x[f][place, :], du_near[:, columns], preferred_element_type=F32)
            mine_ref[slot, k] = held[rows(z), :]
            near_ref[slot, k] = held[rows(z ^ 1), :].astype(BF16)
            mid_ref[slot, k] = held[rows(3 - z), :].astype(BF16)
            far_ref[slot, k] = held[rows(z ^ 2), :].astype(BF16)


def up_products(info, pick_up, own_x, near_x, du_own, du_near, hgroup, blk, chunk):
    factors = len(own_x)
    width, tokens = own_x[0].shape
    count = du_near.shape[1] // blk
    x_spec = pl.BlockSpec((width, tokens), lambda i, *s: (0, 0))
    shape = (factors, count, blk // 4, blk)
    out_spec = pl.BlockSpec(shape, lambda i, *s: (0, 0, 0, 0))
    return pl.pallas_call(
        functools.partial(up_body, factors, count, hgroup, blk, chunk * count),
        grid_spec=pltpu.PrefetchScalarGridSpec(
            num_scalar_prefetch=2,
            grid=(1,),
            in_specs=[x_spec] * (2 * factors)
            + [
                pl.BlockSpec((1, tokens, count * blk), lambda i, *s: (chunk, 0, 0)),
                pl.BlockSpec((tokens, count * blk), lambda i, *s: (0, 0)),
            ],
            out_specs=[out_spec] * 4,
            scratch_shapes=[pltpu.VMEM((blk, blk), F32)],
        ),
        out_shape=[jax.ShapeDtypeStruct(shape, F32)] + [jax.ShapeDtypeStruct(shape, BF16)] * 3,
        compiler_params=pltpu.CompilerParams(vmem_limit_bytes=VMEM_LIMIT),
        cost_estimate=pl.CostEstimate(
            flops=4 * factors * count * blk * blk * tokens,
            bytes_accessed=4 * factors * width * tokens,
            transcendentals=0,
        ),
        name="up_products",
    )(info, pick_up, *own_x, *near_x, du_own, du_near)


def down_body(factors, per_step, hgroup, blk, first, info, pick_down, *refs):
    acts, refs = refs[:4], refs[4:]
    gm_own, refs = refs[0], refs[1:]
    others = [refs[factors * i : factors * (i + 1)] for i in range(3)]
    mine_ref, end_ref = refs[3 * factors :]
    half = blk // 2
    quarter = blk // 4
    odd = info[0] % 2 == 1
    for k in range(per_step):
        j = first + pl.program_id(0) * per_step + k
        rows = slice(k * blk, (k + 1) * blk)
        for f in range(factors):
            slot = info[1 + f]
            place = pl.ds(pl.multiple_of(pick_down[slot * hgroup + j] * half, half), half)
            acc = jnp.dot(acts[0][0, rows, :], gm_own[f, :, place], preferred_element_type=F32)
            for i in range(3):
                acc += jnp.dot(
                    acts[1 + i][rows, :], others[i][f][:, place], preferred_element_type=F32
                )
            low, high = acc[:, :quarter], acc[:, quarter:]
            mine, end = jnp.where(odd, high, low), jnp.where(odd, low, high)
            mine_ref[slot, k] = jnp.concatenate([mine[:half], mine[half:]], axis=1)
            end_ref[slot, k] = jnp.concatenate([end[:half], end[half:]], axis=1).astype(BF16)


def down_products(info, pick_down, act_own, act_others, gm_own, g_others, hgroup, blk, part):
    factors = gm_own.shape[0]
    tokens, half_width = gm_own.shape[1:]
    depth = act_own.shape[1]
    count = depth // blk
    per_step = min(2, count)
    out_shape = (factors, count, blk // 2, blk // 2)
    out_spec = pl.BlockSpec((factors, per_step) + out_shape[2:], lambda i, *s: (0, i, 0, 0))
    g_spec = pl.BlockSpec((tokens, half_width), lambda i, *s: (0, 0))
    return pl.pallas_call(
        functools.partial(down_body, factors, per_step, hgroup, blk, part * count),
        grid_spec=pltpu.PrefetchScalarGridSpec(
            num_scalar_prefetch=2,
            grid=(count // per_step,),
            in_specs=[pl.BlockSpec((1, per_step * blk, tokens), lambda i, *s: (part, i, 0))]
            + [pl.BlockSpec((per_step * blk, tokens), lambda i, *s: (i, 0))] * 3
            + [pl.BlockSpec((factors, tokens, half_width), lambda i, *s: (0, 0, 0))]
            + [g_spec] * (3 * factors),
            out_specs=[out_spec] * 2,
        ),
        out_shape=[jax.ShapeDtypeStruct(out_shape, F32), jax.ShapeDtypeStruct(out_shape, BF16)],
        compiler_params=pltpu.CompilerParams(vmem_limit_bytes=VMEM_LIMIT),
        cost_estimate=pl.CostEstimate(
            flops=4 * factors * count * blk * blk * tokens,
            bytes_accessed=8 * depth * tokens + 8 * factors * tokens * half_width,
            transcendentals=0,
        ),
        name="down_products",
    )(info, pick_down, act_own, *act_others, gm_own, *itertools.chain(*g_others))


def down_finish_body(parts, info, *refs):
    mine, given, out = refs[:parts], refs[parts : 2 * parts], refs[-1]
    middle = info[0] == 1
    quarter = out.shape[-1]
    part = pl.program_id(1)
    for p in range(parts):

        @pl.when(part == p)
        def _():
            value = jnp.where(middle, mine[p][...], given[p][...].astype(F32))
            out[0, :, :, : 2 * quarter, :] = value[:, :, :, :quarter]
            out[0, :, :, 2 * quarter :, :] = value[:, :, :, quarter:]


def down_finish(info, mine, given, blk):
    parts = len(mine)
    factors, count, half, _ = mine[0].shape
    out = (1, factors, parts * count, blk, blk // 4)
    spec = pl.BlockSpec((1, count, half, half), lambda f, p, *s: (f, 0, 0, 0))
    return pl.pallas_call(
        functools.partial(down_finish_body, parts),
        grid_spec=pltpu.PrefetchScalarGridSpec(
            num_scalar_prefetch=1,
            grid=(factors, parts),
            in_specs=[spec] * (2 * parts),
            out_specs=pl.BlockSpec((1, 1, count, blk, blk // 4), lambda f, p, *s: (0, f, p, 0, 0)),
        ),
        out_shape=jax.ShapeDtypeStruct(out, F32),
        compiler_params=pltpu.CompilerParams(vmem_limit_bytes=VMEM_LIMIT),
        name="down_finish",
    )(info, *mine, *given)


def gelu_tanh(values):
    return jax.nn.gelu(values, approximate=True)


def local(acts_in, pre_act, out_grad, up_weight, down_weight, up_pick, down_pick, factor_order):
    bits = lax.axis_size("hid").bit_length() - 1
    factors = bits + 1
    sections = lax.axis_size("section")
    section = lax.axis_index("section")
    z = lax.axis_index("dp")
    middle = jnp.logical_or(z == 1, z == 2)
    micros, tokens, width = acts_in.shape[1:]
    hgroup, blk = up_weight.shape[2], up_weight.shape[-1]
    hidden = hgroup * blk
    rows = micros * tokens
    chunks, parts = 4, 2
    order = factor_order[0]
    pick_up = up_pick.reshape(-1)
    pick_down = down_pick.reshape(-1)
    place = jnp.concatenate([z[None].astype(jnp.int32), order])

    x_own = acts_in[0].reshape(rows, width).T
    x_near = end_to_near(x_own)
    act = gelu_tanh(pre_act[0].astype(F32)).astype(BF16).reshape(rows, hidden).T
    act = act.reshape(parts, hidden // parts, rows)
    act_mid = [mid_swap(act[p]) for p in range(parts)]
    act_near = [end_to_near(act[p]) for p in range(parts)]
    act_far = [mid_swap(act_near[p]) for p in range(parts)]

    du = jnp.zeros((chunks, rows, hidden // chunks), BF16)
    gm = jnp.zeros((factors, rows, width // 2), BF16)
    go = jnp.zeros((rows, width // 2), BF16)
    g_now = [out_grad[m] for m in range(micros)]
    grad = [None] * micros
    x_groups = None
    for step in range(sections):
        active = sections - 1 - step
        here = section == active
        info = jnp.concatenate(
            [jnp.stack([here.astype(jnp.int32), (z // 2).astype(jnp.int32)]), order]
        )
        g_all = [
            [g_now[m]] + [section_partner(g_now[m], bit, active) for bit in range(bits)]
            for m in range(micros)
        ]
        results = []
        for m in range(micros):
            du, gm, go, own, *cross = chain(
                info, pick_up, pick_down, g_all[m], pre_act, down_weight, up_weight, du, gm, go, m, chunks
            )
            total = own
            for bit in range(bits):
                total = total + section_partner(cross[bit], bit, active).astype(F32)
            results.append(total.astype(BF16))
        for m in range(micros):
            grad[m] = results[m] if step == 0 else jnp.where(here, results[m], grad[m])
        if step + 1 < sections:
            g_now = [section_down(results[m], active) for m in range(micros)]
        if x_groups is None:
            x_groups = [
                [value] + [mid_partner(value, bit) for bit in range(bits)] for value in (x_own, x_near)
            ]

    g_near, g_mid, g_far = end_to_near(gm[0]), mid_swap(go), end_to_far(go)
    g_others = [
        [value] + [mid_partner(value, bit) for bit in range(bits)] for value in (g_near, g_mid, g_far)
    ]
    down_mine, down_given = [], []
    for p in range(parts):
        mine, end = down_products(
            place, pick_down, act, (act_near[p], act_mid[p], act_far[p]), gm, g_others, hgroup, blk, p
        )
        down_mine.append(mine)
        down_given.append(near_to_end(end))
    down_grad = down_finish(middle.astype(jnp.int32)[None], down_mine, down_given, blk)

    up_parts = []
    for q in range(chunks):
        du_near = end_to_near(du[q])
        mine, near, mid, far = up_products(
            place, pick_up, x_groups[0], x_groups[1], du, du_near, hgroup, blk, q
        )
        from_near, from_mid, from_far = near_to_end(near), mid_swap(mid), mid_to_far(far)
        up_parts.append(
            jnp.where(
                middle,
                mine + from_mid.astype(F32),
                from_near.astype(F32) + from_far.astype(F32),
            )
        )
    up_grad = jnp.concatenate(up_parts, axis=1)[None]
    grad_in = jnp.stack(grad)[None]
    return grad_in, up_grad, down_grad


def solution(mesh):
    placed = (
        P("section", None, "dp", "hid"),
        P("section", None, "dp", "hid"),
        P(None, "dp", "hid"),
        P("section", None, "hid", None, None),
        P("section", None, "hid", None, None),
        P("section", None, "hid"),
        P("section", None, "hid"),
        P("section", None),
    )
    return jax.shard_map(
        local,
        mesh=mesh,
        in_specs=placed,
        out_specs=(
            P("section", None, "dp", "hid"),
            P("section", None, "hid", "dp", None),
            P("section", None, "hid", None, "dp"),
        ),
        check_vma=False,
    )
```

```python
import functools
import itertools

import jax
import jax.numpy as jnp
from jax import lax
from jax.experimental import pallas as pl
from jax.experimental.pallas import tpu as pltpu
from jax.sharding import PartitionSpec as P

AXES = ("section", "hid", "dp")
VMEM_LIMIT = 52 * 1024 * 1024
ROOT = 0.7978845608028654
CUBE = 0.044715
F32 = jnp.float32
BF16 = jnp.bfloat16


def send(value, target):
    sizes = [lax.axis_size(axis) for axis in AXES]

    def flat(at):
        return (at[0] * sizes[1] + at[1]) * sizes[2] + at[2]

    route = []
    for at in itertools.product(*(range(size) for size in sizes)):
        to = target(*at)
        if to is not None:
            route.append((flat(at), flat(to)))
    return lax.ppermute(value, AXES, route)


def along_dp(value, apart):
    return send(value, lambda s, h, z: (s, h, z ^ apart))


def partner(value, bit):
    return send(value, lambda s, h, z: (s, h ^ 1 << bit, z))


def section_partner(value, bit, active):
    return send(value, lambda s, h, z: (s, h ^ 1 << bit, z) if s == active else None)


def section_down(value, active):
    return send(value, lambda s, h, z: (s - 1, h, z) if s == active else None)


def chain_body(factors, steps, per_step, blk, fgroup, info, pick_up, pick_down, *refs):
    g_refs, refs = refs[:factors], refs[factors:]
    pre_ref, refs = refs[0], refs[1:]
    down_refs, refs = refs[:factors], refs[factors:]
    up_refs, refs = refs[:factors], refs[factors:]
    du_old, keep_old, give_old = refs[:3]
    du_ref, keep_ref, give_ref, own_ref = refs[3:7]
    cross_refs, total = refs[7:-1], refs[-1]
    hgroup = steps * per_step
    half, quarter = blk // 2, blk // 4
    step = pl.program_id(0)
    active = info[0] == 1

    @pl.when(jnp.logical_not(active))
    def _():
        du_ref[...] = du_old[...]

        @pl.when(step == 0)
        def _():
            keep_ref[...] = keep_old[...]
            give_ref[...] = give_old[...]

    @pl.when(active)
    def _():
        @pl.when(step == 0)
        def _():
            total[...] = jnp.zeros_like(total)

            def quarters(ref, at):
                odd = at % 2 == 1
                found = []
                for b in range(fgroup):
                    start = pl.multiple_of(b * blk + at // 2 * half, half)
                    wide = ref[:, pl.ds(start, half)]
                    found.append(jnp.where(odd, wide[:, quarter:], wide[:, :quarter]))
                return jnp.concatenate(found, axis=1)

            for f in range(factors):
                keep_ref[f] = quarters(g_refs[f], info[1])
            for k in range(1, 4):
                give_ref[k - 1] = quarters(g_refs[0], info[1] ^ k)

        for k in range(per_step):
            j = step * per_step + k
            columns = slice(k * blk, (k + 1) * blk)
            da = None
            for f in range(factors):
                pick = pick_down[info[2 + f] * hgroup + j]
                chosen = g_refs[f][:, pl.ds(pl.multiple_of(pick * blk, blk), blk)]
                part = lax.dot_general(
                    chosen, down_refs[f][0, 0, k], (((1,), (1,)), ((), ())), preferred_element_type=F32
                )
                da = part if da is None else da + part
            v = pre_ref[0, 0, :, columns].astype(F32)
            square = v * v
            t = jnp.tanh(ROOT * v * (1.0 + CUBE * square))
            slope = 0.5 * (1.0 + t) + 0.5 * ROOT * v * (1.0 - t * t) * (1.0 + 3.0 * CUBE * square)
            du = (slope * da).astype(BF16)
            du_ref[:, columns] = du
            for f in range(factors):
                pick = pick_up[info[2 + f] * hgroup + j]
                place = pl.ds(pl.multiple_of(pick * blk, blk), blk)
                total[f, :, place] += lax.dot_general(
                    du, up_refs[f][0, 0, k], (((1,), (1,)), ((), ())), preferred_element_type=F32
                )

        @pl.when(step == steps - 1)
        def _():
            own_ref[...] = g_refs[0][...].astype(F32) + total[0]
            for f in range(1, factors):
                cross_refs[f - 1][...] = total[f].astype(BF16)


def chain(info, pick_up, pick_down, g_list, pre_act, down_weight, up_weight, du, keep, give, micro):
    factors = len(g_list)
    tokens, width = g_list[0].shape
    hgroup, blk = up_weight.shape[2], up_weight.shape[-1]
    fgroup = width // blk
    per_step = min(4, hgroup)
    steps = hgroup // per_step
    wide = per_step * blk
    whole = pl.BlockSpec((tokens, width), lambda j, *s: (0, 0))

    def weight_spec(f):
        return pl.BlockSpec(
            (1, 1, per_step, blk, blk), lambda j, info, *s: (0, info[2 + f], j * info[0], 0, 0)
        )

    du_spec = pl.BlockSpec((tokens, wide), lambda j, *s: (micro, j))
    keep_spec = pl.BlockSpec((factors, tokens, width // 4), lambda j, *s: (0, micro, 0))
    give_spec = pl.BlockSpec((3, tokens, width // 4), lambda j, *s: (0, micro, 0))
    pre_spec = pl.BlockSpec((1, 1, tokens, wide), lambda j, info, *s: (0, micro, 0, j * info[0]))
    first_alias = 3 + factors + 1 + 2 * factors
    flat = jax.ShapeDtypeStruct((tokens, width), BF16)
    macs = tokens * hgroup * blk * blk * factors * 2
    return pl.pallas_call(
        functools.partial(chain_body, factors, steps, per_step, blk, fgroup),
        grid_spec=pltpu.PrefetchScalarGridSpec(
            num_scalar_prefetch=3,
            grid=(steps,),
            in_specs=[whole] * factors
            + [pre_spec]
            + [weight_spec(f) for f in range(factors)] * 2
            + [du_spec, keep_spec, give_spec],
            out_specs=[du_spec, keep_spec, give_spec, whole] + [whole] * (factors - 1),
            scratch_shapes=[pltpu.VMEM((factors, tokens, width), F32)],
        ),
        out_shape=[
            jax.ShapeDtypeStruct(du.shape, BF16),
            jax.ShapeDtypeStruct(keep.shape, BF16),
            jax.ShapeDtypeStruct(give.shape, BF16),
            jax.ShapeDtypeStruct((tokens, width), F32),
        ]
        + [flat] * (factors - 1),
        input_output_aliases={first_alias: 0, first_alias + 1: 1, first_alias + 2: 2},
        compiler_params=pltpu.CompilerParams(vmem_limit_bytes=VMEM_LIMIT),
        cost_estimate=pl.CostEstimate(
            flops=2 * macs, bytes_accessed=4 * factors * hgroup * blk * blk, transcendentals=0
        ),
        name="chain",
    )(
        info,
        pick_up,
        pick_down,
        *g_list,
        pre_act,
        *[down_weight] * factors,
        *[up_weight] * factors,
        du,
        keep,
        give,
    )


def up_body(factors, per_step, hgroup, blk, info, pick_up, *refs):
    x_refs, du_ref, out_ref = refs[:factors], refs[factors], refs[factors + 1]
    for k in range(per_step):
        j = pl.program_id(0) * per_step + k
        for f in range(factors):
            slot = info[1 + f]
            place = pl.ds(pl.multiple_of(pick_up[slot * hgroup + j] * blk, blk), blk)
            product = jnp.dot(
                x_refs[f][place, :],
                du_ref[:, k * blk : (k + 1) * blk],
                preferred_element_type=F32,
            )
            out_ref[slot, k] = product.astype(BF16)


def up_products(info, pick_up, x_groups, du, blk):
    factors = len(x_groups)
    width, tokens = x_groups[0].shape
    hgroup = du.shape[1] // blk
    per_step = min(4, hgroup)
    x_spec = pl.BlockSpec((width, tokens), lambda i, *s: (0, 0))
    return pl.pallas_call(
        functools.partial(up_body, factors, per_step, hgroup, blk),
        grid_spec=pltpu.PrefetchScalarGridSpec(
            num_scalar_prefetch=2,
            grid=(hgroup // per_step,),
            in_specs=[x_spec] * factors
            + [pl.BlockSpec((tokens, per_step * blk), lambda i, *s: (0, i))],
            out_specs=pl.BlockSpec((factors, per_step, blk, blk), lambda i, *s: (0, i, 0, 0)),
        ),
        out_shape=jax.ShapeDtypeStruct((factors, hgroup, blk, blk), BF16),
        compiler_params=pltpu.CompilerParams(vmem_limit_bytes=VMEM_LIMIT),
        cost_estimate=pl.CostEstimate(
            flops=2 * factors * hgroup * blk * blk * tokens,
            bytes_accessed=2 * factors * hgroup * blk * blk,
            transcendentals=0,
        ),
        name="up_products",
    )(info, pick_up, *x_groups, du)


def down_body(factors, per_step, hgroup, blk, info, pick_down, act_ref, keep_ref, *refs):
    given, out_ref, turned = refs[:-2], refs[-2], refs[-1]
    quarter = blk // 4
    tokens = act_ref.shape[1]

    @pl.when(pl.program_id(0) == 0)
    def _():
        for f in range(factors):
            for k in range(4):
                source = keep_ref[f] if k == 0 else given[f][k - 1]
                start = pl.multiple_of((info[0] ^ k) * tokens, tokens)
                turned[f, :, pl.ds(start, tokens)] = source.T

    for k in range(per_step):
        j = pl.program_id(0) * per_step + k
        rows = []
        for f in range(factors):
            pick = pick_down[info[1 + f] * hgroup + j]
            rows.append(turned[f, pl.ds(pl.multiple_of(pick * quarter, quarter), quarter), :])
        act = act_ref[:, :, k * blk : (k + 1) * blk].reshape(-1, blk)
        total = jnp.dot(jnp.concatenate(rows, axis=0), act, preferred_element_type=F32)
        for f in range(factors):
            out_ref[0, info[1 + f], k] = total[f * quarter : (f + 1) * quarter]


def down_products(info, pick_down, act_all, keep, given, blk):
    factors = keep.shape[0]
    devices, tokens, hidden = act_all.shape
    quarter_width = keep.shape[-1]
    hgroup = hidden // blk
    per_step = min(2, hgroup)
    return pl.pallas_call(
        functools.partial(down_body, factors, per_step, hgroup, blk),
        grid_spec=pltpu.PrefetchScalarGridSpec(
            num_scalar_prefetch=2,
            grid=(hgroup // per_step,),
            in_specs=[
                pl.BlockSpec((devices, tokens, per_step * blk), lambda i, *s: (0, 0, i)),
                pl.BlockSpec(keep.shape, lambda i, *s: (0, 0, 0)),
            ]
            + [pl.BlockSpec(given[0].shape, lambda i, *s: (0, 0, 0))] * factors,
            out_specs=pl.BlockSpec(
                (1, factors, per_step, blk // 4, blk), lambda i, *s: (0, 0, i, 0, 0)
            ),
            scratch_shapes=[pltpu.VMEM((factors, quarter_width, devices * tokens), BF16)],
        ),
        out_shape=jax.ShapeDtypeStruct((1, factors, hgroup, blk // 4, blk), F32),
        compiler_params=pltpu.CompilerParams(vmem_limit_bytes=VMEM_LIMIT),
        cost_estimate=pl.CostEstimate(
            flops=2 * factors * hgroup * blk * blk * tokens,
            bytes_accessed=2 * devices * tokens * hidden + factors * hgroup * blk * blk,
            transcendentals=0,
        ),
        name="down_products",
    )(info, pick_down, act_all, keep, *given)


def gelu_tanh(values):
    return jax.nn.gelu(values, approximate=True)


def local(acts_in, pre_act, out_grad, up_weight, down_weight, up_pick, down_pick, factor_order):
    bits = lax.axis_size("hid").bit_length() - 1
    factors = bits + 1
    sections = lax.axis_size("section")
    section = lax.axis_index("section")
    z = lax.axis_index("dp").astype(jnp.int32)
    micros, tokens, width = acts_in.shape[1:]
    hgroup, blk = up_weight.shape[2], up_weight.shape[-1]
    hidden = hgroup * blk
    rows = micros * tokens
    order = factor_order[0]
    pick_up = up_pick.reshape(-1)
    pick_down = down_pick.reshape(-1)
    place = jnp.concatenate([z[None], order])

    act = gelu_tanh(pre_act[0].astype(F32)).astype(BF16).reshape(rows, hidden)
    act_all = lax.all_gather(act, "dp")
    x_own = acts_in[0].reshape(rows, width).T

    du = jnp.zeros((rows, hidden), BF16)
    keep = jnp.zeros((factors, rows, width // 4), BF16)
    give = jnp.zeros((3, rows, width // 4), BF16)
    g_now = [out_grad[m] for m in range(micros)]
    grad = [None] * micros
    x_groups = None
    for step in range(sections):
        active = sections - 1 - step
        here = section == active
        info = jnp.concatenate([jnp.stack([here.astype(jnp.int32), z]), order])
        g_all = [
            [g_now[m]] + [section_partner(g_now[m], bit, active) for bit in range(bits)]
            for m in range(micros)
        ]
        results = []
        for m in range(micros):
            du, keep, give, own, *cross = chain(
                info, pick_up, pick_down, g_all[m], pre_act, down_weight, up_weight, du, keep, give, m
            )
            total = own
            for bit in range(bits):
                total = total + section_partner(cross[bit], bit, active).astype(F32)
            results.append(total.astype(BF16))
        for m in range(micros):
            grad[m] = results[m] if step == 0 else jnp.where(here, results[m], grad[m])
        if step + 1 < sections:
            g_now = [section_down(results[m], active) for m in range(micros)]
        if x_groups is None:
            x_groups = [x_own] + [partner(x_own, bit) for bit in range(bits)]

    up_part = up_products(place, pick_up, x_groups, du, blk)
    up_grad = lax.psum_scatter(up_part, "dp", scatter_dimension=2, tiled=True).astype(F32)[None]

    given = jnp.stack([along_dp(give[k - 1], k) for k in range(1, 4)])
    given = [given] + [partner(given, bit) for bit in range(bits)]
    down_grad = down_products(place, pick_down, act_all, keep, given, blk).swapaxes(3, 4)

    return jnp.stack(grad)[None], up_grad, down_grad


def solution(mesh):
    placed = (
        P("section", None, "dp", "hid"),
        P("section", None, "dp", "hid"),
        P(None, "dp", "hid"),
        P("section", None, "hid", None, None),
        P("section", None, "hid", None, None),
        P("section", None, "hid"),
        P("section", None, "hid"),
        P("section", None),
    )
    return jax.shard_map(
        local,
        mesh=mesh,
        in_specs=placed,
        out_specs=(
            P("section", None, "dp", "hid"),
            P("section", None, "hid", "dp", None),
            P("section", None, "hid", None, "dp"),
        ),
        check_vma=False,
    )
```

```python
import functools
import itertools

import jax
import jax.numpy as jnp
from jax import lax
from jax.experimental import pallas as pl
from jax.experimental.pallas import tpu as pltpu
from jax.sharding import PartitionSpec as P

AXES = ("section", "hid", "dp")
VMEM_LIMIT = 30 * 1024 * 1024
CHAIN_LIMIT = 24 * 1024 * 1024
SMALL_LIMIT = 16 * 1024 * 1024
ROOT = 0.7978845608028654
CUBE = 0.044715
F32 = jnp.float32
BF16 = jnp.bfloat16


def send(value, target):
    sizes = [lax.axis_size(axis) for axis in AXES]

    def flat(at):
        return (at[0] * sizes[1] + at[1]) * sizes[2] + at[2]

    route = []
    for at in itertools.product(*(range(size) for size in sizes)):
        to = target(*at)
        if to is not None:
            route.append((flat(at), flat(to)))
    return lax.ppermute(value, AXES, route)


def along_dp(value, apart):
    return send(value, lambda s, h, z: (s, h, z ^ apart))


def partner(value, bit):
    return send(value, lambda s, h, z: (s, h ^ 1 << bit, z))


def section_partner(value, bit, active):
    return send(value, lambda s, h, z: (s, h ^ 1 << bit, z) if s == active else None)


def section_down(value, active):
    return send(value, lambda s, h, z: (s - 1, h, z) if s == active else None)


def slope_of(v):
    square = v * v
    t = jnp.tanh(ROOT * v * (1.0 + CUBE * square))
    return 0.5 * (1.0 + t) + 0.5 * ROOT * v * (1.0 - t * t) * (1.0 + 3.0 * CUBE * square)


def block_of(index, size):
    return pl.ds(pl.multiple_of(index * size, size), size)


def chain_body(cfg, info, pick_up, pick_down, *refs):
    factors, chunks, blk, tokens, micro, terms = cfg
    refs = list(refs)

    def take(count):
        found = refs[:count]
        del refs[:count]
        return found

    g_hbm = take(factors)
    pre_hbm, down_hbm = take(2)
    up_hbm = take(1)[0] if terms else None
    take(1)
    du_hbm = take(1)[0]
    own_ref = take(1)[0] if terms else None
    cross_refs = take(factors - 1) if terms else None
    g_buf, pre_buf, down_buf, du_buf, g_sem, pre_sem, down_sem, du_sem = take(8)
    up_buf, total, up_sem = take(3) if terms else (None,) * 3
    per = down_buf.shape[1] // chunks
    hgroup = per * chunks
    active = info[0] == 1
    half = chunks // 2
    copy = pltpu.make_async_copy

    def g_copy(f):
        return copy(g_hbm[f], g_buf.at[f], g_sem.at[f])

    def weight_copy(hbm, buf, sem, f, c):
        rows = pl.ds(c * per, per)
        return copy(hbm.at[0, info[2 + f], rows], buf.at[f, rows], sem.at[f, c])

    def pre_copy():
        return copy(pre_hbm.at[0, micro], pre_buf, pre_sem)

    def du_copy(c):
        return copy(
            du_buf.at[:, block_of(c, per * blk)],
            du_hbm.at[c // half, pl.ds(micro * tokens, tokens), block_of(c % half, per * blk)],
            du_sem.at[c],
        )

    @pl.when(active)
    def _():
        for f in range(factors):
            g_copy(f).start()
        pre_copy().start()
        for c in range(chunks):
            for f in range(factors):
                weight_copy(down_hbm, down_buf, down_sem, f, c).start()
                if terms:
                    weight_copy(up_hbm, up_buf, up_sem, f, c).start()

    if terms:

        @pl.when(active)
        def _():
            total[...] = jnp.zeros_like(total)

    @pl.when(active)
    def _():
        for f in range(factors):
            g_copy(f).wait()
        pre_copy().wait()

    @pl.loop(0, chunks)
    def _(c):
        @pl.when(active)
        def _():
            for f in range(factors):
                weight_copy(down_hbm, down_buf, down_sem, f, c).wait()
                if terms:
                    weight_copy(up_hbm, up_buf, up_sem, f, c).wait()
            for k in range(per):
                j = c * per + k
                columns = block_of(j, blk)
                da = None
                for f in range(factors):
                    chosen = g_buf[f, :, block_of(pick_down[info[2 + f] * hgroup + j], blk)]
                    part = lax.dot_general(
                        chosen, down_buf[f, j], (((1,), (1,)), ((), ())), preferred_element_type=F32
                    )
                    da = part if da is None else da + part
                du = (slope_of(pre_buf[:, columns].astype(F32)) * da).astype(BF16)
                du_buf[:, columns] = du
                if terms:
                    for f in range(factors):
                        place = block_of(pick_up[info[2 + f] * hgroup + j], blk)
                        total[f, :, place] += lax.dot_general(
                            du, up_buf[f, j], (((1,), (1,)), ((), ())), preferred_element_type=F32
                        )
            du_copy(c).start()

    @pl.when(active)
    def _():
        if terms:
            own_ref[...] = g_buf[0].astype(F32) + total[0]
            for f in range(1, factors):
                cross_refs[f - 1][...] = total[f].astype(BF16)
        for c in range(chunks):
            du_copy(c).wait()


def chain(info, picks, g_list, pre_act, down_weight, up_weight, du, micro, terms):
    factors = len(g_list)
    tokens, width = g_list[0].shape
    hgroup, blk = up_weight.shape[2], up_weight.shape[-1]
    hidden = hgroup * blk
    chunks = min(4, hgroup)
    anywhere = pl.BlockSpec(memory_space=pl.ANY)
    inside = pl.BlockSpec(memory_space=pltpu.VMEM)
    dma = pltpu.SemaphoreType.DMA
    operands = [*g_list, pre_act, down_weight]
    out_shape = [jax.ShapeDtypeStruct(du.shape, BF16)]
    out_specs = [anywhere]
    scratch = [
        pltpu.VMEM((factors, tokens, width), BF16),
        pltpu.VMEM((tokens, hidden), BF16),
        pltpu.VMEM((factors, hgroup, blk, blk), BF16),
        pltpu.VMEM((tokens, hidden), BF16),
        dma((factors,)),
        dma,
        dma((factors, chunks)),
        dma((chunks,)),
    ]
    if terms:
        operands.append(up_weight)
        out_shape.append(jax.ShapeDtypeStruct((tokens, width), F32))
        out_shape += [jax.ShapeDtypeStruct((tokens, width), BF16)] * (factors - 1)
        out_specs += [inside] * factors
        scratch += [
            pltpu.VMEM((factors, hgroup, blk, blk), BF16),
            pltpu.VMEM((factors, tokens, width), F32),
            dma((factors, chunks)),
        ]
    operands.append(du)
    cfg = (factors, chunks, blk, tokens, micro, terms)
    macs = tokens * hgroup * blk * blk * factors * (1 + terms)
    return pl.pallas_call(
        functools.partial(chain_body, cfg),
        grid_spec=pltpu.PrefetchScalarGridSpec(
            num_scalar_prefetch=3,
            grid=(1,),
            in_specs=[anywhere] * len(operands),
            out_specs=out_specs,
            scratch_shapes=scratch,
        ),
        out_shape=out_shape,
        input_output_aliases={3 + len(operands) - 1: 0},
        compiler_params=pltpu.CompilerParams(vmem_limit_bytes=CHAIN_LIMIT),
        cost_estimate=pl.CostEstimate(
            flops=2 * macs,
            bytes_accessed=2 * factors * hgroup * blk * blk * (1 + terms),
            transcendentals=0,
        ),
        name="chain",
    )(info, *picks, *operands)


def terms_body(factors, per_step, hgroup, blk, info, pick_up, g_ref, du_ref, *refs):
    up_refs, own_ref = refs[:factors], refs[factors]
    cross_refs, total = refs[factors + 1 : -1], refs[-1]
    step = pl.program_id(0)

    @pl.when(info[0] == 1)
    def _():
        @pl.when(step == 0)
        def _():
            total[...] = jnp.zeros_like(total)

        for k in range(per_step):
            du = du_ref[0, :, k * blk : (k + 1) * blk]
            for f in range(factors):
                pick = pick_up[info[2 + f] * hgroup + step * per_step + k]
                total[f, :, block_of(pick, blk)] += lax.dot_general(
                    du, up_refs[f][0, 0, k], (((1,), (1,)), ((), ())), preferred_element_type=F32
                )

        @pl.when(step == pl.num_programs(0) - 1)
        def _():
            own_ref[...] = g_ref[...].astype(F32) + total[0]
            for f in range(1, factors):
                cross_refs[f - 1][...] = total[f].astype(BF16)


def last_terms(info, pick_up, g, du, up_weight):
    factors, hgroup, blk = up_weight.shape[1], up_weight.shape[2], up_weight.shape[-1]
    rows, width = g.shape
    per_step = min(4, hgroup // 2)
    half = hgroup // 2 // per_step
    whole = pl.BlockSpec((rows, width), lambda j, *s: (0, 0))

    def weight_spec(f):
        return pl.BlockSpec(
            (1, 1, per_step, blk, blk), lambda j, info, *s: (0, info[2 + f], j * info[0], 0, 0)
        )

    return pl.pallas_call(
        functools.partial(terms_body, factors, per_step, hgroup, blk),
        grid_spec=pltpu.PrefetchScalarGridSpec(
            num_scalar_prefetch=2,
            grid=(hgroup // per_step,),
            in_specs=[
                whole,
                pl.BlockSpec((1, rows, per_step * blk), lambda j, *s: (j // half, 0, j % half)),
            ]
            + [weight_spec(f) for f in range(factors)],
            out_specs=[whole] * factors,
            scratch_shapes=[pltpu.VMEM((factors, rows, width), F32)],
        ),
        out_shape=[jax.ShapeDtypeStruct((rows, width), F32)]
        + [jax.ShapeDtypeStruct((rows, width), BF16)] * (factors - 1),
        compiler_params=pltpu.CompilerParams(vmem_limit_bytes=VMEM_LIMIT),
        cost_estimate=pl.CostEstimate(
            flops=2 * rows * hgroup * blk * blk * factors,
            bytes_accessed=2 * factors * hgroup * blk * blk,
            transcendentals=0,
        ),
        name="last_terms",
    )(info, pick_up, g, du, *[up_weight] * factors)


def select_body(blk, tokens, info, *refs):
    quarter = blk // 4
    sources, keep_ref, give_ref, turned = refs[:-3], refs[-3], refs[-2], refs[-1]
    for m, ref in enumerate(sources):
        columns = slice(m * tokens, (m + 1) * tokens)
        for b in range(ref.shape[1] // blk):
            turned[...] = ref[:, b * blk : (b + 1) * blk].T
            for i, out in enumerate((keep_ref, keep_ref, give_ref, give_ref)):
                start = b * blk // 2 + i % 2 * quarter
                out[start : start + quarter, columns] = turned[block_of(info[i], quarter), :]


def select(wanted, sources, blk):
    tokens, width = sources[0].shape
    inside = pl.BlockSpec(memory_space=pltpu.VMEM)
    return pl.pallas_call(
        functools.partial(select_body, blk, tokens),
        grid_spec=pltpu.PrefetchScalarGridSpec(
            num_scalar_prefetch=1,
            grid=(1,),
            in_specs=[inside] * len(sources),
            out_specs=[inside] * 2,
            scratch_shapes=[pltpu.VMEM((blk, tokens), BF16)],
        ),
        out_shape=[jax.ShapeDtypeStruct((width // 2, len(sources) * tokens), BF16)] * 2,
        compiler_params=pltpu.CompilerParams(vmem_limit_bytes=SMALL_LIMIT),
        name="select",
    )(wanted, *sources)


def products_body(factors, per_step, hgroup, blk, first, info, picks, own_ref, other_ref, *refs):
    lefts, keep_ref, send_ref = refs[:factors], refs[factors], refs[factors + 1]
    half, quarter = blk // 2, blk // 4
    for k in range(per_step):
        j = first + pl.program_id(0) * per_step + k
        columns = slice(k * blk, (k + 1) * blk)
        rights = own_ref[0, :, columns], other_ref[0, :, columns]
        for f in range(factors):
            slot = info[1 + f]
            rows = block_of(picks[slot * hgroup + j], half)
            total = jnp.dot(lefts[f][0, rows, :], rights[0], preferred_element_type=F32)
            total += jnp.dot(lefts[f][1, rows, :], rights[1], preferred_element_type=F32)
            keep_ref[slot, k] = total[:quarter]
            send_ref[slot, k] = total[quarter:].astype(BF16)


def products(info, picks, lefts, own, part, pair, hgroup, blk, first):
    factors = len(lefts)
    tokens, hidden = own.shape[1:]
    count = hidden // blk
    per_step = min(4, count)
    shape = (factors, count, blk // 4, blk)
    out_spec = pl.BlockSpec((factors, per_step) + shape[2:], lambda i, *s: (0, i, 0, 0))
    return pl.pallas_call(
        functools.partial(products_body, factors, per_step, hgroup, blk, first),
        grid_spec=pltpu.PrefetchScalarGridSpec(
            num_scalar_prefetch=2,
            grid=(count // per_step,),
            in_specs=[
                pl.BlockSpec((1, tokens, per_step * blk), lambda i, *s: (part, 0, i)),
                pl.BlockSpec((1, tokens, per_step * blk), lambda i, info, *s: (info[0], 0, i)),
            ]
            + [pl.BlockSpec(lefts[0].shape, lambda i, *s: (0, 0, 0))] * factors,
            out_specs=[out_spec] * 2,
        ),
        out_shape=[jax.ShapeDtypeStruct(shape, F32), jax.ShapeDtypeStruct(shape, BF16)],
        compiler_params=pltpu.CompilerParams(vmem_limit_bytes=VMEM_LIMIT),
        cost_estimate=pl.CostEstimate(
            flops=2 * factors * count * blk * blk * tokens,
            bytes_accessed=4 * tokens * hidden + 3 * factors * count * blk * blk,
            transcendentals=0,
        ),
        name="products",
    )(info, picks, own, pair, *lefts)


def gelu_tanh(values):
    return jax.nn.gelu(values, approximate=True)


def after(value, *earlier):
    return lax.optimization_barrier((value, earlier))[0]


def local(acts_in, pre_act, out_grad, up_weight, down_weight, up_pick, down_pick, factor_order):
    bits = lax.axis_size("hid").bit_length() - 1
    sections = lax.axis_size("section")
    section = lax.axis_index("section")
    z = lax.axis_index("dp").astype(jnp.int32)
    micros, tokens, width = acts_in.shape[1:]
    hgroup, blk = up_weight.shape[2], up_weight.shape[-1]
    hidden = hgroup * blk
    rows = micros * tokens
    order = factor_order[0]
    picks = up_pick.reshape(-1), down_pick.reshape(-1)

    def exchanged(value, active):
        return [value] + [section_partner(value, bit, active) for bit in range(bits)]

    def groups(value):
        return [value] + [partner(value, bit) for bit in range(bits)]

    act = gelu_tanh(pre_act[0].astype(F32)).astype(BF16).reshape(1, rows, hidden)
    act_pair = lax.all_gather(act[0], "dp", axis_index_groups=[[0, 3], [1, 2]])
    x_keep, x_give = select(jnp.stack([z, z ^ 3, z ^ 1, z ^ 2]), [acts_in[0].reshape(rows, width)], blk)
    x_came = along_dp(x_give, 1)

    g_now = [out_grad[m] for m in range(micros)]
    g_layer = list(g_now)
    grad = [None] * micros
    du = jnp.zeros((2, rows, hidden // 2), BF16)
    for step in range(sections):
        active = sections - 1 - step
        here = section == active
        info = jnp.concatenate([jnp.stack([here.astype(jnp.int32), z]), order])
        g_all = [exchanged(g_now[m], active) for m in range(micros)]
        if step:
            g_layer = [jnp.where(here, g_now[m], g_layer[m]) for m in range(micros)]
        if step == sections - 1:
            break
        results = []
        for m in range(micros):
            du, own, *cross = chain(
                info, picks, g_all[m], pre_act, down_weight, up_weight, du, m, True
            )
            total = own
            for bit in range(bits):
                total = total + section_partner(cross[bit], bit, active).astype(F32)
            results.append(total.astype(BF16))
        grad = [results[m] if step == 0 else jnp.where(here, results[m], grad[m]) for m in range(micros)]
        g_now = [section_down(results[m], active) for m in range(micros)]
        if step == 0:
            x_groups = groups(after(jnp.stack([x_keep, x_came]), du))
    g_keep, g_give = select(jnp.stack([z, z ^ 1, z ^ 3, z ^ 2]), g_layer, blk)
    g_came = along_dp(g_give, 3)
    for m in range(micros):
        (du,) = chain(info, picks, g_all[m], pre_act, down_weight, up_weight, du, m, False)

    du, act_pair = lax.optimization_barrier((du, act_pair))
    place = jnp.concatenate([0 * z[None], order])
    up_grad = []
    for part in range(2):
        du_pair = along_dp(du[part], 1)[None]
        keep, give = products(
            place, picks[0], x_groups, du, part, du_pair, hgroup, blk, part * hgroup // 2
        )
        up_grad.append(keep + along_dp(give, 3).astype(F32))
    up_grad = jnp.concatenate(up_grad, axis=1)[None]

    g_groups = groups(after(jnp.stack([g_keep, g_came]), du))
    place = jnp.concatenate([1 - z[None] // 2, order])
    keep, give = products(place, picks[1], g_groups, act, 0, act_pair, hgroup, blk, 0)
    down_grad = (keep + along_dp(give, 1).astype(F32))[None].swapaxes(3, 4)

    own, *cross = last_terms(info, picks[0], jnp.concatenate(g_now, axis=0), du, up_weight)
    for bit in range(bits):
        own = own + section_partner(cross[bit], bit, active).astype(F32)
    result = own.astype(BF16).reshape(micros, tokens, width)
    grad_in = jnp.where(here, result, jnp.stack(grad))[None]
    return grad_in, up_grad, down_grad


def solution(mesh):
    placed = (
        P("section", None, "dp", "hid"),
        P("section", None, "dp", "hid"),
        P(None, "dp", "hid"),
        P("section", None, "hid", None, None),
        P("section", None, "hid", None, None),
        P("section", None, "hid"),
        P("section", None, "hid"),
        P("section", None),
    )
    return jax.shard_map(
        local,
        mesh=mesh,
        in_specs=placed,
        out_specs=(
            P("section", None, "dp", "hid"),
            P("section", None, "hid", "dp", None),
            P("section", None, "hid", None, "dp"),
        ),
        check_vma=False,
    )
```

```python
import functools
import itertools

import jax
import jax.numpy as jnp
from jax import lax
from jax.experimental import pallas as pl
from jax.experimental.pallas import tpu as pltpu
from jax.sharding import PartitionSpec as P

AXES = ("section", "hid", "dp")
VMEM_LIMIT = 30 * 1024 * 1024
CHAIN_LIMIT = 24 * 1024 * 1024
SMALL_LIMIT = 16 * 1024 * 1024
ROOT = 0.7978845608028654
CUBE = 0.044715
F32 = jnp.float32
BF16 = jnp.bfloat16


def send(value, target):
    sizes = [lax.axis_size(axis) for axis in AXES]

    def flat(at):
        return (at[0] * sizes[1] + at[1]) * sizes[2] + at[2]

    route = []
    for at in itertools.product(*(range(size) for size in sizes)):
        to = target(*at)
        if to is not None:
            route.append((flat(at), flat(to)))
    return lax.ppermute(value, AXES, route)


def along_dp(value, apart):
    return send(value, lambda s, h, z: (s, h, z ^ apart))


def partner(value, bit):
    return send(value, lambda s, h, z: (s, h ^ 1 << bit, z))


def section_partner(value, bit, active):
    return send(value, lambda s, h, z: (s, h ^ 1 << bit, z) if s == active else None)


def section_down(value, active):
    return send(value, lambda s, h, z: (s - 1, h, z) if s == active else None)


def slope_of(v):
    square = v * v
    t = jnp.tanh(ROOT * v * (1.0 + CUBE * square))
    return 0.5 * (1.0 + t) + 0.5 * ROOT * v * (1.0 - t * t) * (1.0 + 3.0 * CUBE * square)


def block_of(index, size):
    return pl.ds(pl.multiple_of(index * size, size), size)


def chain_body(cfg, info, pick_up, pick_down, *refs):
    factors, chunks, blk, tokens, micro, terms = cfg
    refs = list(refs)

    def take(count):
        found = refs[:count]
        del refs[:count]
        return found

    g_hbm = take(factors)
    pre_hbm, down_hbm = take(2)
    up_hbm = take(1)[0] if terms else None
    take(1)
    du_hbm = take(1)[0]
    own_ref = take(1)[0] if terms else None
    cross_refs = take(factors - 1) if terms else None
    g_buf, pre_buf, down_buf, du_buf, g_sem, pre_sem, down_sem, du_sem = take(8)
    up_buf, total, up_sem = take(3) if terms else (None,) * 3
    per = down_buf.shape[1] // chunks
    hgroup = per * chunks
    active = info[0] == 1
    half = chunks // 2
    copy = pltpu.make_async_copy

    def g_copy(f):
        return copy(g_hbm[f], g_buf.at[f], g_sem.at[f])

    def weight_copy(hbm, buf, sem, f, c):
        rows = pl.ds(c * per, per)
        return copy(hbm.at[0, info[2 + f], rows], buf.at[f, rows], sem.at[f, c])

    def pre_copy():
        return copy(pre_hbm.at[0, micro], pre_buf, pre_sem)

    def du_copy(c):
        return copy(
            du_buf.at[:, block_of(c, per * blk)],
            du_hbm.at[c // half, pl.ds(micro * tokens, tokens), block_of(c % half, per * blk)],
            du_sem.at[c],
        )

    @pl.when(active)
    def _():
        for f in range(factors):
            g_copy(f).start()
        pre_copy().start()
        for c in range(chunks):
            for f in range(factors):
                weight_copy(down_hbm, down_buf, down_sem, f, c).start()
                if terms:
                    weight_copy(up_hbm, up_buf, up_sem, f, c).start()

    if terms:

        @pl.when(active)
        def _():
            total[...] = jnp.zeros_like(total)

    @pl.when(active)
    def _():
        for f in range(factors):
            g_copy(f).wait()
        pre_copy().wait()

    @pl.loop(0, chunks)
    def _(c):
        @pl.when(active)
        def _():
            for f in range(factors):
                weight_copy(down_hbm, down_buf, down_sem, f, c).wait()
                if terms:
                    weight_copy(up_hbm, up_buf, up_sem, f, c).wait()
            for k in range(per):
                j = c * per + k
                columns = block_of(j, blk)
                da = None
                for f in range(factors):
                    chosen = g_buf[f, :, block_of(pick_down[info[2 + f] * hgroup + j], blk)]
                    part = lax.dot_general(
                        chosen, down_buf[f, j], (((1,), (1,)), ((), ())), preferred_element_type=F32
                    )
                    da = part if da is None else da + part
                du = (slope_of(pre_buf[:, columns].astype(F32)) * da).astype(BF16)
                du_buf[:, columns] = du
                if terms:
                    for f in range(factors):
                        place = block_of(pick_up[info[2 + f] * hgroup + j], blk)
                        total[f, :, place] += lax.dot_general(
                            du, up_buf[f, j], (((1,), (1,)), ((), ())), preferred_element_type=F32
                        )
            du_copy(c).start()

    @pl.when(active)
    def _():
        if terms:
            own_ref[...] = g_buf[0].astype(F32) + total[0]
            for f in range(1, factors):
                cross_refs[f - 1][...] = total[f].astype(BF16)
        for c in range(chunks):
            du_copy(c).wait()


def chain(info, picks, g_list, pre_act, down_weight, up_weight, du, micro, terms):
    factors = len(g_list)
    tokens, width = g_list[0].shape
    hgroup, blk = up_weight.shape[2], up_weight.shape[-1]
    hidden = hgroup * blk
    chunks = min(4, hgroup)
    anywhere = pl.BlockSpec(memory_space=pl.ANY)
    inside = pl.BlockSpec(memory_space=pltpu.VMEM)
    dma = pltpu.SemaphoreType.DMA
    operands = [*g_list, pre_act, down_weight]
    out_shape = [jax.ShapeDtypeStruct(du.shape, BF16)]
    out_specs = [anywhere]
    scratch = [
        pltpu.VMEM((factors, tokens, width), BF16),
        pltpu.VMEM((tokens, hidden), BF16),
        pltpu.VMEM((factors, hgroup, blk, blk), BF16),
        pltpu.VMEM((tokens, hidden), BF16),
        dma((factors,)),
        dma,
        dma((factors, chunks)),
        dma((chunks,)),
    ]
    if terms:
        operands.append(up_weight)
        out_shape.append(jax.ShapeDtypeStruct((tokens, width), F32))
        out_shape += [jax.ShapeDtypeStruct((tokens, width), BF16)] * (factors - 1)
        out_specs += [inside] * factors
        scratch += [
            pltpu.VMEM((factors, hgroup, blk, blk), BF16),
            pltpu.VMEM((factors, tokens, width), F32),
            dma((factors, chunks)),
        ]
    operands.append(du)
    cfg = (factors, chunks, blk, tokens, micro, terms)
    macs = tokens * hgroup * blk * blk * factors * (1 + terms)
    return pl.pallas_call(
        functools.partial(chain_body, cfg),
        grid_spec=pltpu.PrefetchScalarGridSpec(
            num_scalar_prefetch=3,
            grid=(1,),
            in_specs=[anywhere] * len(operands),
            out_specs=out_specs,
            scratch_shapes=scratch,
        ),
        out_shape=out_shape,
        input_output_aliases={3 + len(operands) - 1: 0},
        compiler_params=pltpu.CompilerParams(vmem_limit_bytes=CHAIN_LIMIT),
        cost_estimate=pl.CostEstimate(
            flops=2 * macs,
            bytes_accessed=2 * factors * hgroup * blk * blk * (1 + terms),
            transcendentals=0,
        ),
        name="chain",
    )(info, *picks, *operands)


def terms_body(factors, per_step, hgroup, blk, info, pick_up, g_ref, du_ref, *refs):
    up_refs, own_ref = refs[:factors], refs[factors]
    cross_refs, total = refs[factors + 1 : -1], refs[-1]
    step = pl.program_id(0)

    @pl.when(info[0] == 1)
    def _():
        @pl.when(step == 0)
        def _():
            total[...] = jnp.zeros_like(total)

        for k in range(per_step):
            du = du_ref[0, :, k * blk : (k + 1) * blk]
            for f in range(factors):
                pick = pick_up[info[2 + f] * hgroup + step * per_step + k]
                total[f, :, block_of(pick, blk)] += lax.dot_general(
                    du, up_refs[f][0, 0, k], (((1,), (1,)), ((), ())), preferred_element_type=F32
                )

        @pl.when(step == pl.num_programs(0) - 1)
        def _():
            own_ref[...] = g_ref[...].astype(F32) + total[0]
            for f in range(1, factors):
                cross_refs[f - 1][...] = total[f].astype(BF16)


def last_terms(info, pick_up, g, du, up_weight):
    factors, hgroup, blk = up_weight.shape[1], up_weight.shape[2], up_weight.shape[-1]
    rows, width = g.shape
    per_step = min(4, hgroup // 2)
    half = hgroup // 2 // per_step
    whole = pl.BlockSpec((rows, width), lambda j, *s: (0, 0))

    def weight_spec(f):
        return pl.BlockSpec(
            (1, 1, per_step, blk, blk), lambda j, info, *s: (0, info[2 + f], j * info[0], 0, 0)
        )

    return pl.pallas_call(
        functools.partial(terms_body, factors, per_step, hgroup, blk),
        grid_spec=pltpu.PrefetchScalarGridSpec(
            num_scalar_prefetch=2,
            grid=(hgroup // per_step,),
            in_specs=[
                whole,
                pl.BlockSpec((1, rows, per_step * blk), lambda j, *s: (j // half, 0, j % half)),
            ]
            + [weight_spec(f) for f in range(factors)],
            out_specs=[whole] * factors,
            scratch_shapes=[pltpu.VMEM((factors, rows, width), F32)],
        ),
        out_shape=[jax.ShapeDtypeStruct((rows, width), F32)]
        + [jax.ShapeDtypeStruct((rows, width), BF16)] * (factors - 1),
        compiler_params=pltpu.CompilerParams(vmem_limit_bytes=VMEM_LIMIT),
        cost_estimate=pl.CostEstimate(
            flops=2 * rows * hgroup * blk * blk * factors,
            bytes_accessed=2 * factors * hgroup * blk * blk,
            transcendentals=0,
        ),
        name="last_terms",
    )(info, pick_up, g, du, *[up_weight] * factors)


def select_body(blk, tokens, info, *refs):
    quarter = blk // 4
    sources, keep_ref, give_ref, turned = refs[:-3], refs[-3], refs[-2], refs[-1]
    for m, ref in enumerate(sources):
        columns = slice(m * tokens, (m + 1) * tokens)
        for b in range(ref.shape[1] // blk):
            turned[...] = ref[:, b * blk : (b + 1) * blk].T
            for i, out in enumerate((keep_ref, keep_ref, give_ref, give_ref)):
                start = b * blk // 2 + i % 2 * quarter
                out[start : start + quarter, columns] = turned[block_of(info[i], quarter), :]


def select(wanted, sources, blk):
    tokens, width = sources[0].shape
    inside = pl.BlockSpec(memory_space=pltpu.VMEM)
    return pl.pallas_call(
        functools.partial(select_body, blk, tokens),
        grid_spec=pltpu.PrefetchScalarGridSpec(
            num_scalar_prefetch=1,
            grid=(1,),
            in_specs=[inside] * len(sources),
            out_specs=[inside] * 2,
            scratch_shapes=[pltpu.VMEM((blk, tokens), BF16)],
        ),
        out_shape=[jax.ShapeDtypeStruct((width // 2, len(sources) * tokens), BF16)] * 2,
        compiler_params=pltpu.CompilerParams(vmem_limit_bytes=SMALL_LIMIT),
        name="select",
    )(wanted, *sources)


def products_body(factors, per_step, hgroup, blk, first, info, picks, own_ref, other_ref, *refs):
    lefts, keep_ref, send_ref = refs[:factors], refs[factors], refs[factors + 1]
    half, quarter = blk // 2, blk // 4
    for k in range(per_step):
        j = first + pl.program_id(0) * per_step + k
        columns = slice(k * blk, (k + 1) * blk)
        rights = own_ref[0, :, columns], other_ref[0, :, columns]
        for f in range(factors):
            slot = info[1 + f]
            rows = block_of(picks[slot * hgroup + j], half)
            total = jnp.dot(lefts[f][0, rows, :], rights[0], preferred_element_type=F32)
            total += jnp.dot(lefts[f][1, rows, :], rights[1], preferred_element_type=F32)
            keep_ref[slot, k] = total[:quarter]
            send_ref[slot, k] = total[quarter:].astype(BF16)


def products(info, picks, lefts, own, part, pair, hgroup, blk, first):
    factors = len(lefts)
    tokens, hidden = own.shape[1:]
    count = hidden // blk
    per_step = min(4, count)
    shape = (factors, count, blk // 4, blk)
    out_spec = pl.BlockSpec((factors, per_step) + shape[2:], lambda i, *s: (0, i, 0, 0))
    return pl.pallas_call(
        functools.partial(products_body, factors, per_step, hgroup, blk, first),
        grid_spec=pltpu.PrefetchScalarGridSpec(
            num_scalar_prefetch=2,
            grid=(count // per_step,),
            in_specs=[
                pl.BlockSpec((1, tokens, per_step * blk), lambda i, *s: (part, 0, i)),
                pl.BlockSpec((1, tokens, per_step * blk), lambda i, info, *s: (info[0], 0, i)),
            ]
            + [pl.BlockSpec(lefts[0].shape, lambda i, *s: (0, 0, 0))] * factors,
            out_specs=[out_spec] * 2,
        ),
        out_shape=[jax.ShapeDtypeStruct(shape, F32), jax.ShapeDtypeStruct(shape, BF16)],
        compiler_params=pltpu.CompilerParams(vmem_limit_bytes=VMEM_LIMIT),
        cost_estimate=pl.CostEstimate(
            flops=2 * factors * count * blk * blk * tokens,
            bytes_accessed=4 * tokens * hidden + 3 * factors * count * blk * blk,
            transcendentals=0,
        ),
        name="products",
    )(info, picks, own, pair, *lefts)


def gelu_tanh(values):
    return jax.nn.gelu(values, approximate=True)


def after(value, *earlier):
    return lax.optimization_barrier((value, earlier))[0]


def local(acts_in, pre_act, out_grad, up_weight, down_weight, up_pick, down_pick, factor_order):
    bits = lax.axis_size("hid").bit_length() - 1
    sections = lax.axis_size("section")
    section = lax.axis_index("section")
    z = lax.axis_index("dp").astype(jnp.int32)
    micros, tokens, width = acts_in.shape[1:]
    hgroup, blk = up_weight.shape[2], up_weight.shape[-1]
    hidden = hgroup * blk
    rows = micros * tokens
    order = factor_order[0]
    picks = up_pick.reshape(-1), down_pick.reshape(-1)

    def exchanged(value, active):
        return [value] + [section_partner(value, bit, active) for bit in range(bits)]

    def groups(value):
        return [value] + [partner(value, bit) for bit in range(bits)]

    act = gelu_tanh(pre_act[0].astype(F32)).astype(BF16).reshape(1, rows, hidden)
    act_pair = lax.all_gather(act[0], "dp", axis_index_groups=[[0, 3], [1, 2]])
    x_keep, x_give = select(jnp.stack([z, z ^ 3, z ^ 1, z ^ 2]), [acts_in[0].reshape(rows, width)], blk)
    x_came = along_dp(x_give, 1)

    g_now = [out_grad[m] for m in range(micros)]
    g_layer = list(g_now)
    grad = [None] * micros
    du = jnp.zeros((2, rows, hidden // 2), BF16)
    for step in range(sections):
        active = sections - 1 - step
        here = section == active
        info = jnp.concatenate([jnp.stack([here.astype(jnp.int32), z]), order])
        g_all = [exchanged(g_now[m], active) for m in range(micros)]
        if step:
            g_layer = [jnp.where(here, g_now[m], g_layer[m]) for m in range(micros)]
        if step == sections - 1:
            break
        results = []
        for m in range(micros):
            du, own, *cross = chain(
                info, picks, g_all[m], pre_act, down_weight, up_weight, du, m, True
            )
            total = own
            for bit in range(bits):
                total = total + section_partner(cross[bit], bit, active).astype(F32)
            results.append(total.astype(BF16))
        grad = [results[m] if step == 0 else jnp.where(here, results[m], grad[m]) for m in range(micros)]
        g_now = [section_down(results[m], active) for m in range(micros)]
    g_keep, g_give = select(jnp.stack([z, z ^ 1, z ^ 3, z ^ 2]), g_layer, blk)
    g_came = along_dp(g_give, 3)
    for m in range(micros):
        (du,) = chain(info, picks, g_all[m], pre_act, down_weight, up_weight, du, m, False)
        if m == 0:
            x_groups = groups(after(jnp.stack([x_keep, x_came]), du))

    du, act_pair = lax.optimization_barrier((du, act_pair))
    place = jnp.concatenate([0 * z[None], order])
    up_grad = []
    for part in range(2):
        du_pair = along_dp(du[part], 1)[None]
        keep, give = products(
            place, picks[0], x_groups, du, part, du_pair, hgroup, blk, part * hgroup // 2
        )
        up_grad.append(keep + along_dp(give, 3).astype(F32))
    up_grad = jnp.concatenate(up_grad, axis=1)[None]

    g_groups = groups(after(jnp.stack([g_keep, g_came]), du))
    place = jnp.concatenate([1 - z[None] // 2, order])
    keep, give = products(place, picks[1], g_groups, act, 0, act_pair, hgroup, blk, 0)
    down_grad = (keep + along_dp(give, 1).astype(F32))[None].swapaxes(3, 4)

    own, *cross = last_terms(info, picks[0], jnp.concatenate(g_now, axis=0), du, up_weight)
    for bit in range(bits):
        own = own + section_partner(cross[bit], bit, active).astype(F32)
    result = own.astype(BF16).reshape(micros, tokens, width)
    grad_in = jnp.where(here, result, jnp.stack(grad))[None]
    return grad_in, up_grad, down_grad


def solution(mesh):
    placed = (
        P("section", None, "dp", "hid"),
        P("section", None, "dp", "hid"),
        P(None, "dp", "hid"),
        P("section", None, "hid", None, None),
        P("section", None, "hid", None, None),
        P("section", None, "hid"),
        P("section", None, "hid"),
        P("section", None),
    )
    return jax.shard_map(
        local,
        mesh=mesh,
        in_specs=placed,
        out_specs=(
            P("section", None, "dp", "hid"),
            P("section", None, "hid", "dp", None),
            P("section", None, "hid", None, "dp"),
        ),
        check_vma=False,
    )
```
